256 devices in a mesh: ctx: 4 (over x), head: 32 (over z, y), rep: 2 (over core).
Axes of the slice: x: 4, y: 4, z: 8, core: 2. Of those that a mesh axis runs over, the one named last changes fastest.
Arguments:
- queries: bfloat16 [1024, 16384], P(('rep', 'ctx'), 'head'), parts along dimension 0, may hold values from -16 to 16
- history_keys: bfloat16 [32768, 1024], P(('rep', 'ctx')), parts along dimension 0, may hold values from -8 to 8
- history_values: bfloat16 [32768, 1024], P(('rep', 'ctx')), parts along dimension 0, may hold values from -6 to 6
- new_keys: bfloat16 [1024, 1024], P(('rep', 'ctx')), parts along dimension 0, may hold values from -6 to 6
- new_values: bfloat16 [1024, 1024], P(('rep', 'ctx')), parts along dimension 0, may hold values from -6 to 6
- shard_lengths: int32 [8], P(('rep', 'ctx')), parts along dimension 0, may hold values from 1 to 4096, 10240 in all
- positions: int32 [1024], P('rep'), parts along dimension 0, may hold values from 0 to 511, each once
- out_weight: bfloat16 [16384, 16384], P('head', 'ctx'), may hold values from -0.75 to 0.75
Outputs:
- mixed: bfloat16 [1024, 16384], P(('rep', 'head'), 'ctx'), parts along dimension 0
The draws below stay inside these ranges and needn't reach their ends.
There are 2 independent parts, one for each index of `rep`. The reference program is written for one: setup_inputs(seed, part) draws one part's arguments, and reference() takes and returns one part's arrays. A program takes and returns all parts, laid end to end along the dimension named above; an argument that names none is the same for every part. Nothing has to cross between parts.
All inputs are finite; a program needn't handle non-finite values. No bound on the sum of `shard_lengths` on one device may be relied on, other than what follows from the above.
Results may differ from the reference program's by a relative error of at most 0.0054.
Values may be sent and summed in bfloat16 or wider, within the bound.
No kernel may reach another device: no remote copies, remote signals or barrier semaphores. Data moves between devices by JAX's collectives and lax.ppermute only.
A program may use at most 128 MiB of HBM per device.

```python
import math
import jax
import jax.numpy as jnp
import numpy as np
from jax import lax

D = 16384
HD = 128
GROUP = 16
KVH = 8
QTOK_DEV = 128
HIST_DEV = 4096
TILE = 512
QTOK = 512
HIST = 16384
HIST_LIVE = 10240
N_CTX = 4


def draw_queries(key, part):
    key = jax.random.fold_in(key, 11)
    feature_count = KVH * GROUP * HD
    values = 2.0 * jax.random.normal(key, (QTOK, feature_count), jnp.float32)
    return jnp.clip(values, -16.0, 16.0).astype(jnp.bfloat16)


def draw_history_keys(key, part):
    key = jax.random.fold_in(key, 23)
    feature_count = KVH * HD
    values = jax.random.normal(key, (HIST, feature_count), jnp.float32)
    return jnp.clip(values, -8.0, 8.0).astype(jnp.bfloat16)


def steps_of(own_key, dims, pieces, smallest, largest):
    def one(position, parts):
        steps = jax.random.uniform(jax.random.fold_in(jax.random.fold_in(own_key, 6), position), (parts,), jnp.float32, smallest / len(pieces), largest / len(pieces))
        return jnp.repeat(jnp.exp(steps), dims[position] // parts).reshape((-1,) + (1,) * (len(dims) - position - 1))

    level = one(*pieces[0])
    for cut in pieces[1:]:
        level = level * one(*cut)
    return level


def split_up(number_of, total, reach, slope):
    loads = [(1 << 20) // math.isqrt(rank ** slope) + 1 for rank in range(2, number_of + 1)]
    spare, given = total - reach - (number_of - 1), [1] * (number_of - 1)
    while spare > 0:
        movable = [i for i in range(number_of - 1) if given[i] < reach]
        mass, remaining = sum([loads[i] for i in movable]), spare
        for i in movable:
            addition = min(reach - given[i], max(1, remaining * loads[i] // mass), spare)
            given[i] = given[i] + addition
            spare = spare - addition
    return np.array([reach] + given)


def uneven(own_key, amount, total, limit, slope):
    if amount == 2:
        one = jax.random.randint(own_key, (), max(1, total - limit), min(limit, total - 1) + 1)
        return jnp.stack([one, total - one])
    tallies = jnp.asarray(split_up(amount, total, limit, slope), jnp.int32)
    twos = (amount - 1) // 2
    donor, taker = tallies[1:1 + 2 * twos:2], tallies[2:2 + 2 * twos:2]
    margin = jnp.minimum(donor - 1, limit - taker)
    moved = jax.random.randint(jax.random.fold_in(own_key, 1), (twos,), 0, 1 << 20) % (margin + 1)
    tallies = tallies.at[1:1 + 2 * twos:2].set(donor - moved).at[2:2 + 2 * twos:2].set(taker + moved)
    return tallies[jax.random.permutation(jax.random.fold_in(own_key, 2), amount)]


def scatter_about(rng, extent, deviation, limit, pieces=(), kind=jnp.bfloat16):
    entries = jax.random.normal(rng, extent, jnp.float32) * deviation
    if len(pieces) > 0:
        entries = steps_of(rng, extent, pieces, -0.22, 0.18) * entries
    return jnp.clip(entries, min=-limit, max=limit).astype(kind)


def setup_inputs(seed: int = 0, part: int = 0) -> dict:
    key_list = jax.random.split(jax.random.key(seed), 9)
    own_keys = jax.random.split(jax.random.fold_in(key_list[8], part), 9)
    return {
        "queries": draw_queries(jax.random.fold_in(jax.random.fold_in(key_list[8], part), 71), part),
        "history_keys": draw_history_keys(jax.random.fold_in(jax.random.fold_in(key_list[8], part), 71), part),
        "history_values": scatter_about(own_keys[2], (HIST, KVH * HD), 1.0, 6.0, ((0, 4),)),
        "new_keys": scatter_about(own_keys[3], (QTOK, KVH * HD), 1.0, 6.0, ((0, 4),)),
        "new_values": scatter_about(own_keys[4], (QTOK, KVH * HD), 1.0, 6.0, ((0, 4),)),
        "shard_lengths": uneven(own_keys[5], N_CTX, HIST_LIVE, HIST_DEV, 2).astype(jnp.int32),
        "positions": jax.random.permutation(own_keys[6], QTOK).astype(jnp.int32),
        "out_weight": scatter_about(key_list[7], (KVH * GROUP * HD, D), (KVH * GROUP * HD // 256) ** -0.5, 0.75, ((0, 32), (1, 4))),
    }


neg_fill = -1.0e30


def block_terms(queried, key_block, value_block, visible):
    scores = jnp.einsum("qjd,kd->qjk", queried.astype(jnp.float32), key_block.astype(jnp.float32)) * (HD ** -0.5)
    key_mask = visible[:, None, :]
    scores = jnp.where(key_mask, scores, neg_fill)
    block_top = jnp.max(scores, axis=-1)
    weights = jnp.where(key_mask, jnp.exp(scores - block_top[..., None]), 0.0).astype(jnp.bfloat16)
    block_sum = jnp.sum(weights.astype(jnp.float32), axis=-1)
    block_out = jnp.einsum("qjk,kd->qjd", weights.astype(jnp.float32), value_block.astype(jnp.float32))
    return block_out, block_top, block_sum


def combine_states(first, second):
    out_a, top_a, sum_a = first
    out_b, top_b, sum_b = second
    peak_top = jnp.maximum(top_a, top_b)
    scale_a = jnp.exp(top_a - peak_top)
    scale_b = jnp.exp(top_b - peak_top)
    return (out_a * scale_a[..., None] + out_b * scale_b[..., None], peak_top, sum_a * scale_a + sum_b * scale_b)


def reference(queries, history_keys, history_values, new_keys, new_values, shard_lengths, positions, out_weight):
    slot_ids = jnp.arange(HIST, dtype=jnp.int32)
    live_slots = (slot_ids % HIST_DEV) < shard_lengths[slot_ids // HIST_DEV]
    live_tiles = live_slots.reshape(HIST // TILE, TILE)
    new_pos = positions.reshape(N_CTX, QTOK_DEV)
    per_query = queries.reshape(QTOK, KVH, GROUP, HD).transpose(1, 0, 2, 3)
    per_hkeys = history_keys.reshape(HIST, KVH, HD).transpose(1, 0, 2)
    per_hvals = history_values.reshape(HIST, KVH, HD).transpose(1, 0, 2)
    per_nkeys = new_keys.reshape(QTOK, KVH, HD).transpose(1, 0, 2)
    per_nvals = new_values.reshape(QTOK, KVH, HD).transpose(1, 0, 2)

    def one_head(inputs):
        queried, hkeys, hvals, nkeys, nvals = inputs
        initial = (jnp.zeros((QTOK, GROUP, HD), jnp.float32), jnp.full((QTOK, GROUP), neg_fill, jnp.float32), jnp.zeros((QTOK, GROUP), jnp.float32))

        def hist_step(carried, tile_inputs):
            key_tile, value_tile, live_tile = tile_inputs
            return combine_states(carried, block_terms(queried, key_tile, value_tile, live_tile[None, :])), None

        carried, _ = lax.scan(hist_step, initial, (hkeys.reshape(HIST // TILE, TILE, HD), hvals.reshape(HIST // TILE, TILE, HD), live_tiles))

        def new_step(carried, tile_inputs):
            key_tile, value_tile, pos_tile = tile_inputs
            visible = pos_tile[None, :] <= positions[:, None]
            return combine_states(carried, block_terms(queried, key_tile, value_tile, visible)), None

        carried, _ = lax.scan(new_step, carried, (nkeys.reshape(N_CTX, QTOK_DEV, HD), nvals.reshape(N_CTX, QTOK_DEV, HD), new_pos))
        total_out, total_top, total_sum = carried
        return (total_out / total_sum[..., None]).astype(jnp.bfloat16)

    attended = lax.map(one_head, (per_query, per_hkeys, per_hvals, per_nkeys, per_nvals))
    attention = attended.transpose(1, 0, 2, 3).reshape(QTOK, KVH * GROUP * HD)
    return jnp.dot(attention, out_weight, preferred_element_type=jnp.float32).astype(jnp.bfloat16)
```

```python
import functools

import jax
import jax.numpy as jnp
from jax import lax
from jax.experimental import pallas as pl
from jax.experimental.pallas import tpu as pltpu
from jax.sharding import Mesh
from jax.sharding import PartitionSpec as P

HD = 128
GROUP = 16
NEG = -1e30
VMEM = 56 << 20


def shift(x, axis, size, by):
    return lax.ppermute(x, axis, [(i, (i + by) % size) for i in range(size)])


def attn_kernel(blocks, first, tok, heads, tile, steps, n_ctx, scalars, *refs):
    q_refs = refs[:blocks]
    k_ref, v_ref, nk_ref, nv_ref, pos_ref = refs[blocks : blocks + 5]
    outs = refs[blocks + 5 : 2 * blocks + 5]
    q_s, top_s, acc_s = refs[2 * blocks + 5 :]
    step = pl.program_id(0)
    live = scalars[0]
    ctx = scalars[2]
    rows = tok * heads

    @pl.when(step == 0)
    def _():
        for b in range(blocks):
            for h in range(heads):
                q_s[pl.ds(b * rows + h * tok, tok), :] = q_refs[b][:, h * HD : (h + 1) * HD]
        top_s[...] = jnp.full(top_s.shape, NEG, jnp.float32)
        acc_s[...] = jnp.zeros(acc_s.shape, jnp.float32)

    def add(b, keys, values, mask):
        own = pl.ds(b * rows, rows)
        scores = lax.dot_general(
            q_s[own, :], keys, (((1,), (1,)), ((), ())), preferred_element_type=jnp.float32
        )
        scores = scores * (HD**-0.5)
        if mask is not None:
            scores = jnp.where(mask(b, scores.shape), scores, NEG)
        old = top_s[own, :]
        new = jnp.maximum(old, jnp.max(scores, axis=1, keepdims=True))
        weights = jnp.exp(scores - new[:, :1]).astype(jnp.bfloat16)
        scale = jnp.exp(old - new)
        both = jnp.concatenate([values, jnp.ones_like(values)], axis=1)
        part = jnp.dot(weights, both, preferred_element_type=jnp.float32)
        acc_s[own, :] = acc_s[own, :] * jnp.concatenate([scale, scale], axis=1) + part
        top_s[own, :] = new

    @pl.when((step + 1) * tile <= live)
    def _():
        for b in range(blocks):
            add(b, k_ref[...], v_ref[...], None)

    @pl.when(((step + 1) * tile > live) & (step * tile < live))
    def _():
        def mask(b, shape):
            return step * tile + lax.broadcasted_iota(jnp.int32, shape, 1) < live

        for b in range(blocks):
            add(b, k_ref[...], v_ref[...], mask)

    @pl.when(step == steps - 1)
    def _():
        key_pos = jnp.broadcast_to(pos_ref[pl.ds(ctx, 1), :], (tok, tok))

        def mask(b, shape):
            row = pos_ref[pl.ds(lax.rem(ctx + n_ctx - first - b, n_ctx), 1), :]
            seen = key_pos <= jnp.broadcast_to(row, (tok, tok)).T
            return jnp.concatenate([seen] * heads, axis=0)

        for b in range(blocks):
            add(b, nk_ref[...], nv_ref[...], mask)
        lane = lax.broadcasted_iota(jnp.int32, (tok, HD), 1)
        for b in range(blocks):
            stats = jnp.zeros((tok, HD), jnp.float32)
            for h in range(heads):
                own = pl.ds(b * rows + h * tok, tok)
                total = acc_s[own, HD:]
                outs[b][:, h * HD : (h + 1) * HD] = (acc_s[own, :HD] / total).astype(jnp.bfloat16)
                level = top_s[own, :] + jnp.log(total)
                high = level.astype(jnp.bfloat16).astype(jnp.float32)
                middle = (level - high).astype(jnp.bfloat16).astype(jnp.float32)
                low = level - high - middle
                stats = jnp.where(lane == 3 * h, high, stats)
                stats = jnp.where(lane == 3 * h + 1, middle, stats)
                stats = jnp.where(lane == 3 * h + 2, low, stats)
            outs[b][:, heads * HD :] = stats.astype(jnp.bfloat16)


def attend(queries, first, keys, values, new_keys, new_values, pos, scalars):
    blocks = len(queries)
    tok, width = queries[0].shape
    heads = width // HD
    tile = min(2048, keys.shape[0])
    steps = keys.shape[0] // tile
    n_ctx = pos.shape[0]
    whole = lambda shape: pl.BlockSpec(shape, lambda i, s: (0, 0))
    hist = pl.BlockSpec((tile, HD), lambda i, s: (jnp.minimum(i, (s[0] - 1) // tile), s[1]))
    new = pl.BlockSpec((new_keys.shape[0], HD), lambda i, s: (0, s[1]))
    total = blocks * tok * heads
    return pl.pallas_call(
        functools.partial(attn_kernel, blocks, first, tok, heads, tile, steps, n_ctx),
        grid_spec=pltpu.PrefetchScalarGridSpec(
            num_scalar_prefetch=1,
            grid=(steps,),
            in_specs=[whole((tok, width))] * blocks + [hist, hist, new, new, whole(pos.shape)],
            out_specs=[whole((tok, width + HD))] * blocks,
            scratch_shapes=[
                pltpu.VMEM((total, HD), jnp.bfloat16),
                pltpu.VMEM((total, HD), jnp.float32),
                pltpu.VMEM((total, 2 * HD), jnp.float32),
            ],
        ),
        out_shape=[jax.ShapeDtypeStruct((tok, width + HD), jnp.bfloat16)] * blocks,
        compiler_params=pltpu.CompilerParams(vmem_limit_bytes=VMEM),
        cost_estimate=pl.CostEstimate(
            flops=8 * total * keys.shape[0] * HD,
            bytes_accessed=4 * keys.shape[0] * HD,
            transcendentals=total * keys.shape[0],
        ),
        name="attend",
    )(scalars, *queries, keys, values, new_keys, new_values, pos)


def combine_kernel(heads, *refs):
    parts, outs = refs[:-2], refs[-2:]
    tok = parts[0].shape[0]
    for h in range(heads):
        at = heads * HD + 3 * h
        levels = []
        for p in parts:
            pieces = p[:, heads * HD :].astype(jnp.float32)
            j = 3 * h
            level = pieces[:, j : j + 1] + pieces[:, j + 1 : j + 2] + pieces[:, j + 2 : j + 3]
            levels.append(jnp.broadcast_to(level, (tok, HD)))
        top = functools.reduce(jnp.maximum, levels)
        weights = [jnp.exp(level - top) for level in levels]
        total = sum(weights[1:], weights[0])
        own = slice(h * HD, (h + 1) * HD)
        mixed = sum(w * p[:, own].astype(jnp.float32) for w, p in zip(weights, parts))
        done = (mixed / total).astype(jnp.bfloat16)
        outs[0][:, own] = done[: tok // 2]
        outs[1][:, own] = done[tok // 2 :]


def combine(parts):
    tok, width = parts[0].shape
    width -= HD
    return pl.pallas_call(
        functools.partial(combine_kernel, width // HD),
        out_shape=[jax.ShapeDtypeStruct((tok // 2, width), jnp.bfloat16)] * 2,
        compiler_params=pltpu.CompilerParams(vmem_limit_bytes=VMEM),
        name="combine",
    )(*parts)


def project_kernel(n_ctx, n_y, half, scalars, *refs):
    a_refs = refs[:n_y]
    b_refs = refs[n_y : n_y + n_ctx]
    own_ref, near_ref, far_ref, out_ref = refs[n_y + n_ctx :]
    ctx, core = scalars[2], scalars[4]
    feat = own_ref.shape[0]
    cut = feat // 2
    acc = None

    def left(t, cols):
        pieces = [a_refs[t][:, cols]]
        pieces += [b[pl.ds(t * half, half), cols] for b in b_refs]
        return jnp.concatenate(pieces, axis=0)

    def add(acc, lhs, rhs):
        prod = jnp.dot(lhs, rhs, preferred_element_type=jnp.float32)
        return prod if acc is None else acc + prod

    acc = add(acc, left(0, slice(None)), own_ref[...])
    for t in range(1, n_y):
        rows = slice((t - 1) * cut, t * cut)
        mine = pl.ds(pl.multiple_of(core * cut, cut), cut)
        other = pl.ds(pl.multiple_of((1 - core) * cut, cut), cut)
        acc = add(acc, left(t, mine), near_ref[rows, :])
        acc = add(acc, left(t, other), far_ref[rows, :])
    acc = acc.astype(out_ref.dtype)
    for s in range(n_ctx):
        at = lax.rem(ctx + n_ctx - s, n_ctx) * (2 * half)
        for second in range(2):
            piece = (second * n_ctx + s) * half
            place = pl.ds(pl.multiple_of(at + second * half, half), half)
            out_ref[place, :] = acc[piece : piece + half]


def project(a_parts, b_parts, own, near, far, scalars):
    n_y, n_ctx = len(a_parts), len(b_parts)
    rows, feat = a_parts[0].shape
    half = rows // n_ctx
    cols = own.shape[1]
    tile = min(256, cols)
    whole = pl.BlockSpec((rows, feat), lambda i, s: (0, 0))
    other = pl.BlockSpec(b_parts[0].shape, lambda i, s: (0, 0))
    strip = lambda x: pl.BlockSpec((x.shape[0], tile), lambda i, s: (0, i))
    out_rows = 2 * half * n_ctx
    return pl.pallas_call(
        functools.partial(project_kernel, n_ctx, n_y, half),
        grid_spec=pltpu.PrefetchScalarGridSpec(
            num_scalar_prefetch=1,
            grid=(cols // tile,),
            in_specs=[whole] * n_y + [other] * n_ctx + [strip(own), strip(near), strip(far)],
            out_specs=pl.BlockSpec((out_rows, tile), lambda i, s: (0, i)),
        ),
        out_shape=jax.ShapeDtypeStruct((out_rows, cols), jnp.bfloat16),
        compiler_params=pltpu.CompilerParams(vmem_limit_bytes=VMEM),
        cost_estimate=pl.CostEstimate(
            flops=2 * out_rows * feat * n_y * cols, bytes_accessed=7 << 20, transcendentals=0
        ),
        name="project",
    )(scalars, *a_parts, *b_parts, own, near, far)


def shards(
    sizes,
    queries,
    history_keys,
    history_values,
    new_keys,
    new_values,
    shard_lengths,
    positions,
    out_weight,
):
    n_ctx, n_z, n_y, n_rep = sizes
    ctx, z, y, core = (lax.axis_index(a) for a in ("ctx", "z", "y", "rep"))
    kv_head = (z * n_y + y) * (queries.shape[1] // HD) // GROUP
    scalars = jnp.stack([shard_lengths[0], kv_head, ctx, y, core]).astype(jnp.int32)
    pos = positions.reshape(n_ctx, -1)

    feat, all_cols = out_weight.shape
    cols = all_cols // n_y
    cut = feat // n_rep
    with jax.named_scope("weights"):
        near = []
        for t in range(1, n_y):
            to = lax.rem(y + t, n_y)
            block = lax.dynamic_slice(out_weight, (core * cut, to * cols), (cut, cols))
            near.append(shift(block, "y", n_y, t))
        near = jnp.concatenate(near, axis=0)
        far = shift(near, "rep", n_rep, 1)
        own = lax.dynamic_slice(out_weight, (0, y * cols), (feat, cols))

    history = (history_keys, history_values, new_keys, new_values, pos, scalars)
    with jax.named_scope("queries"):
        others = [shift(queries, "ctx", n_ctx, s) for s in range(1, n_ctx)]
    with jax.named_scope("attend"):
        (kept,) = attend([queries], 0, *history)
        sent = attend(others, 1, *history)
    with jax.named_scope("return"):
        back = [shift(p, "ctx", n_ctx, -s) for s, p in enumerate(sent, 1)]
        first, second = combine([kept] + back)
    with jax.named_scope("gather"):
        a = jnp.concatenate(
            [first] + [shift(first, "ctx", n_ctx, s) for s in range(1, n_ctx)], axis=0
        )
        b = jnp.concatenate([second] + [shift(second, "y", n_y, t) for t in range(1, n_y)], axis=0)
        a_parts = [a] + [shift(a, "y", n_y, t) for t in range(1, n_y)]
        b_parts = [b] + [shift(b, "ctx", n_ctx, s) for s in range(1, n_ctx)]
    with jax.named_scope("project"):
        part = project(a_parts, b_parts, own, near, far, scalars)
    with jax.named_scope("reduce"):
        got = lax.all_to_all(part, ("z", "y"), 0, 0, tiled=True)
        got = got.reshape(n_z, n_y, -1, cols).astype(jnp.float32)
        mixed = jnp.sum(got, axis=0).astype(jnp.bfloat16)
        return mixed.transpose(1, 0, 2).reshape(-1, all_cols)


def solution(mesh):
    n_ctx, n_head, n_rep = (mesh.shape[a] for a in ("ctx", "head", "rep"))
    n_y = n_ctx
    n_z = n_head // n_y
    devices = mesh.devices.reshape(n_ctx, n_z, n_y, n_rep)
    fine = Mesh(devices, ("ctx", "z", "y", "rep"))
    head = ("z", "y")
    in_specs = (
        P(("rep", "ctx"), head),
        P(("rep", "ctx"), None),
        P(("rep", "ctx"), None),
        P(("rep", "ctx"), None),
        P(("rep", "ctx"), None),
        P(("rep", "ctx")),
        P("rep"),
        P(head, "ctx"),
    )
    return jax.shard_map(
        functools.partial(shards, (n_ctx, n_z, n_y, n_rep)),
        mesh=fine,
        in_specs=in_specs,
        out_specs=P(("rep", head[0], head[1]), "ctx"),
        check_vma=False,
    )
```

```python
import functools

import jax
import jax.numpy as jnp
from jax import lax
from jax.experimental import pallas as pl
from jax.experimental.pallas import tpu as pltpu
from jax.sharding import Mesh
from jax.sharding import PartitionSpec as P

HD = 128
GROUP = 16
NEG = -1e30
SCALE2 = HD**-0.5 * 1.4426950408889634
VMEM = 60 << 20
EXTRA = 16


def shift(x, axis, size, by):
    return lax.ppermute(x, axis, [(i, (i + by) % size) for i in range(size)])


def attn_kernel(blocks, begin, tok, heads, tile, chunk, n_ctx, scalars, *refs):
    q_refs = refs[:blocks]
    k_hbm, v_hbm, nk_hbm, nv_hbm, pos_ref = refs[blocks : blocks + 5]
    outs = refs[blocks + 5 : 2 * blocks + 5]
    q_s, top_s, acc_s, k_s, v_s, nk_s, nv_s, sem, new_sem = refs[2 * blocks + 5 : 2 * blocks + 14]
    buffers = refs[2 * blocks + 14 : 2 * blocks + 17], refs[2 * blocks + 17 :]
    live, kv_head, ctx = scalars[0], scalars[1], scalars[2]
    rows = tok * heads
    total = blocks * rows
    chunks = total // chunk
    steps = k_s.shape[0] // tile
    lanes = pl.ds(pl.multiple_of(kv_head * HD, HD), HD)
    tiles = (live + tile - 1) // tile
    full = live // tile

    new_copies = [
        pltpu.make_async_copy(nk_hbm.at[:, lanes], nk_s, new_sem.at[0]),
        pltpu.make_async_copy(nv_hbm.at[:, lanes], nv_s, new_sem.at[1]),
    ]

    def tile_copies(i):
        at = pl.ds(i * tile, tile)
        return [
            pltpu.make_async_copy(k_hbm.at[at, lanes], k_s.at[at, :], sem.at[0, i]),
            pltpu.make_async_copy(v_hbm.at[at, lanes], v_s.at[at, :], sem.at[1, i]),
        ]

    for copy in new_copies:
        copy.start()
    for i in range(steps):

        @pl.when(i < tiles)
        def _():
            for copy in tile_copies(i):
                copy.start()

    for b in range(blocks):
        for h in range(heads):
            q_s[pl.ds(b * rows + h * tok, tok), :] = q_refs[b][:, h * HD : (h + 1) * HD]
    for copy in new_copies:
        copy.wait()

    def score(own, keys):
        return lax.dot_general(
            q_s[own, :], keys, (((1,), (1,)), ((), ())), preferred_element_type=jnp.float32
        )

    def weigh(weights, values):
        both = jnp.concatenate([values, jnp.ones_like(values)], axis=1)
        return jnp.dot(weights.astype(jnp.bfloat16), both, preferred_element_type=jnp.float32)

    key_pos = jnp.broadcast_to(pos_ref[pl.ds(ctx, 1), :], (tok, tok))
    def start(b, carry):
        row = pos_ref[pl.ds(lax.rem(ctx + n_ctx - begin - b, n_ctx), 1), :]
        seen = key_pos <= jnp.broadcast_to(row, (tok, tok)).T
        seen = jnp.concatenate([seen] * heads, axis=0)
        own = pl.ds(pl.multiple_of(b * rows, rows), rows)
        scores = jnp.where(seen, score(own, nk_s[...]), NEG)
        top = jnp.max(scores, axis=1, keepdims=True)
        weights = jnp.where(seen, jnp.exp2((scores - top) * SCALE2), 0.0)
        acc_s[own, :] = weigh(weights, nv_s[...])
        top_s[own, :] = jnp.broadcast_to(top, (rows, HD))
        return carry

    lax.fori_loop(0, blocks, start, 0)

    def place(n):
        i = n // chunks
        c = n - i * chunks
        return (
            pl.ds(pl.multiple_of(c * chunk, chunk), chunk),
            pl.ds(pl.multiple_of(i * tile, tile), tile),
        )

    def first(n, buffer, masked=False):
        score_b, top_b, scale_b = buffer
        own, keys = place(n)
        scores = score(own, k_s[keys, :])
        if masked:
            slot = full * tile + lax.broadcasted_iota(jnp.int32, scores.shape, 1)
            scores = jnp.where(slot < live, scores, NEG)
        score_b[...] = scores
        old = top_s[own, :]
        new = jnp.maximum(old, jnp.max(scores, axis=1, keepdims=True))
        scale_b[...] = jnp.exp2((old - new) * SCALE2)
        top_b[...] = new
        top_s[own, :] = new

    def second(n, buffer):
        score_b, top_b, scale_b = buffer
        own, keys = place(n)
        weights = jnp.exp2((score_b[...] - top_b[:, :1]) * SCALE2)
        part = weigh(weights, v_s[keys, :])
        scale = scale_b[...]
        acc_s[own, :] = acc_s[own, :] * jnp.concatenate([scale, scale], axis=1) + part

    for i in range(steps):

        @pl.when(i < tiles)
        def _():
            for copy in tile_copies(i):
                copy.wait()

    def sweep(start, count, masked):
        first(start, buffers[0], masked)

        def pair(j, carry):
            n = start + 2 * j
            first(n + 1, buffers[1], masked)
            second(n, buffers[0])
            first(jnp.where(2 * j + 2 < count, n + 2, start), buffers[0], masked)
            second(n + 1, buffers[1])
            return carry

        lax.fori_loop(0, count // 2, pair, 0)

    @pl.when(full > 0)
    def _():
        sweep(0, full * chunks, False)

    @pl.when(full < tiles)
    def _():
        sweep(full * chunks, chunks, True)

    lane = lax.broadcasted_iota(jnp.int32, (tok, HD), 1)
    for b in range(blocks):
        stats = jnp.zeros((tok, HD), jnp.float32)
        for h in range(heads):
            own = pl.ds(b * rows + h * tok, tok)
            sums = acc_s[own, HD:]
            done = (acc_s[own, :HD] / sums).astype(jnp.bfloat16)
            outs[b][:tok, h * HD : (h + 1) * HD] = done
            level = top_s[own, :] * HD**-0.5 + jnp.log(sums)
            high = level.astype(jnp.bfloat16).astype(jnp.float32)
            middle = (level - high).astype(jnp.bfloat16).astype(jnp.float32)
            low = level - high - middle
            stats = jnp.where(lane == 3 * h, high, stats)
            stats = jnp.where(lane == 3 * h + 1, middle, stats)
            stats = jnp.where(lane == 3 * h + 2, low, stats)
        turned = stats.T[:EXTRA].astype(jnp.bfloat16)
        outs[b][tok:, :] = jnp.concatenate([turned] * heads, axis=1)


def attend(queries, begin, keys, values, new_keys, new_values, pos, scalars):
    blocks = len(queries)
    tok, width = queries[0].shape
    heads = width // HD
    slots = keys.shape[0]
    total = blocks * tok * heads
    tile = slots
    chunk = min(256, total // 2)
    vmem = pl.BlockSpec(memory_space=pltpu.VMEM)
    hbm = pl.BlockSpec(memory_space=pltpu.HBM)
    f32, b16 = jnp.float32, jnp.bfloat16
    buffer = [pltpu.VMEM((chunk, tile), f32)] + [pltpu.VMEM((chunk, HD), f32)] * 2
    return pl.pallas_call(
        functools.partial(attn_kernel, blocks, begin, tok, heads, tile, chunk, pos.shape[0]),
        in_specs=[pl.BlockSpec(memory_space=pltpu.SMEM)] + [vmem] * blocks + [hbm] * 4 + [vmem],
        out_specs=[vmem] * blocks,
        scratch_shapes=[
            pltpu.VMEM((total, HD), b16),
            pltpu.VMEM((total, HD), f32),
            pltpu.VMEM((total, 2 * HD), f32),
            pltpu.VMEM((slots, HD), b16),
            pltpu.VMEM((slots, HD), b16),
            pltpu.VMEM((new_keys.shape[0], HD), b16),
            pltpu.VMEM((new_keys.shape[0], HD), b16),
            pltpu.SemaphoreType.DMA((2, slots // tile)),
            pltpu.SemaphoreType.DMA((2,)),
        ]
        + buffer * 2,
        out_shape=[jax.ShapeDtypeStruct((tok + EXTRA, width), b16)] * blocks,
        compiler_params=pltpu.CompilerParams(vmem_limit_bytes=VMEM),
        cost_estimate=pl.CostEstimate(
            flops=8 * total * slots * HD, bytes_accessed=4 * slots * HD, transcendentals=total * slots
        ),
        name="attend",
    )(scalars, *queries, keys, values, new_keys, new_values, pos)


def combine_kernel(copies, spans, *refs):
    parts, out_ref = refs[:-1], refs[-1]
    tok = parts[0].shape[0] - EXTRA
    width = parts[0].shape[1]
    piece = lax.broadcasted_iota(jnp.int32, (EXTRA, width), 0)
    head = lax.broadcasted_iota(jnp.int32, (EXTRA, width), 1) // HD
    spread = ((piece >= 3 * head) & (piece < 3 * head + 3)).astype(jnp.float32).astype(jnp.bfloat16)
    levels = [
        lax.dot_general(
            p[tok:, :tok], spread, (((0,), (0,)), ((), ())), preferred_element_type=jnp.float32
        )
        for p in parts
    ]
    top = functools.reduce(jnp.maximum, levels)
    weights = [jnp.exp(level - top) for level in levels]
    total = sum(weights[1:], weights[0])
    mixed = sum(w * p[:tok, :].astype(jnp.float32) for w, p in zip(weights, parts))
    done = (mixed / total).astype(jnp.bfloat16)
    piece = tok // (2 * spans)
    for k in range(copies):
        for n in range(spans):
            at = (2 * n + k // 2 % 2) * piece
            to = (k * spans + n) * piece
            out_ref[to : to + piece, :] = done[at : at + piece]


def combine(parts, copies, spans):
    tok, width = parts[0].shape
    tok -= EXTRA
    vmem = pl.BlockSpec(memory_space=pltpu.VMEM)
    return pl.pallas_call(
        functools.partial(combine_kernel, copies, spans),
        in_specs=[vmem] * len(parts),
        out_specs=vmem,
        out_shape=jax.ShapeDtypeStruct((copies * tok // 2, width), jnp.bfloat16),
        compiler_params=pltpu.CompilerParams(vmem_limit_bytes=VMEM),
        name="combine",
    )(*parts)


def cut_kernel(scalars, weight, one_ref, two_ref, sem):
    side, core = scalars[3] % 2, scalars[4]
    cut, cols = two_ref.shape
    other = pl.ds(pl.multiple_of((1 - side) * cols, cols), cols)
    same = pl.ds(pl.multiple_of(side * cols, cols), cols)
    rows = pl.ds(pl.multiple_of(core * cut, cut), cut)
    copies = [
        pltpu.make_async_copy(weight.at[:, other], one_ref, sem.at[0]),
        pltpu.make_async_copy(weight.at[rows, same], two_ref, sem.at[1]),
    ]
    for copy in copies:
        copy.start()
    for copy in copies:
        copy.wait()


def cut_weight(weight, scalars):
    feat, cols = weight.shape
    vmem = pl.BlockSpec(memory_space=pltpu.VMEM)
    return pl.pallas_call(
        cut_kernel,
        in_specs=[
            pl.BlockSpec(memory_space=pltpu.SMEM),
            pl.BlockSpec(memory_space=pltpu.HBM),
        ],
        out_specs=[vmem, vmem],
        scratch_shapes=[pltpu.SemaphoreType.DMA((2,))],
        out_shape=[
            jax.ShapeDtypeStruct((feat, cols // 2), weight.dtype),
            jax.ShapeDtypeStruct((feat // 2, cols // 2), weight.dtype),
        ],
        compiler_params=pltpu.CompilerParams(vmem_limit_bytes=VMEM),
        cost_estimate=pl.CostEstimate(flops=0, bytes_accessed=1, transcendentals=0),
        name="cut",
    )(scalars, weight)


def mark_kernel(after, out_ref):
    out_ref[...] = jnp.zeros_like(out_ref)


def mark(after, flops):
    return pl.pallas_call(
        mark_kernel,
        in_specs=[pl.BlockSpec(memory_space=pl.ANY)],
        out_specs=pl.BlockSpec(memory_space=pltpu.VMEM),
        out_shape=jax.ShapeDtypeStruct((8, HD), jnp.float32),
        cost_estimate=pl.CostEstimate(flops=flops, bytes_accessed=0, transcendentals=0),
        name="mark",
    )(after)


def project_kernel(n_ctx, n_y, scalars, got_ref, weight, *refs):
    near, far, near_half, far_half, _, out_ref, rhs_s, acc_s, sem = refs
    y, core = scalars[3], scalars[4]
    feat, cols = near.shape
    cut = feat // 2
    lanes = pl.ds(pl.multiple_of(y % 2 * cols, cols), cols)
    one = pl.ds(pl.multiple_of(core * cut, cut), cut)
    two = pl.ds(pl.multiple_of((1 - core) * cut, cut), cut)
    first = jnp.where(core == 0, 1, 3)
    groups = [
        (y, [(weight.at[:, lanes], rhs_s.at[0])]),
        (y ^ 2, [(near_half, rhs_s.at[1, one, :]), (far_half, rhs_s.at[1, two, :])]),
        (y ^ first, [(near, rhs_s.at[2])]),
        (y ^ (4 - first), [(far, rhs_s.at[3])]),
    ]
    copies = [
        [pltpu.make_async_copy(a, b, sem.at[t, k]) for k, (a, b) in enumerate(group)]
        for t, (_, group) in enumerate(groups)
    ]
    for group in copies:
        for copy in group:
            copy.start()
    for t, (src, _) in enumerate(groups):
        lhs = jnp.concatenate([got_ref[c * n_y + src] for c in range(n_ctx)], axis=0)
        for copy in copies[t]:
            copy.wait()

        part = jnp.dot(lhs, rhs_s[t], preferred_element_type=jnp.float32)
        if t == 0:
            acc_s[...] = part
        elif t < n_y - 1:
            acc_s[...] += part
        else:
            out_ref[...] = (acc_s[...] + part).astype(out_ref.dtype)


def project(got, weight, pieces, n_ctx, n_y, scalars, after):
    blocks, tok, feat = got.shape
    cols = pieces[0].shape[1]
    rows = n_ctx * tok
    vmem = pl.BlockSpec(memory_space=pltpu.VMEM)
    hbm = pl.BlockSpec(memory_space=pltpu.HBM)
    return pl.pallas_call(
        functools.partial(project_kernel, n_ctx, n_y),
        in_specs=[pl.BlockSpec(memory_space=pltpu.SMEM), vmem] + [hbm] * (1 + len(pieces))
        + [pl.BlockSpec(memory_space=pl.ANY)],
        out_specs=vmem,
        scratch_shapes=[
            pltpu.VMEM((n_y, feat, cols), jnp.bfloat16),
            pltpu.VMEM((rows, cols), jnp.float32),
            pltpu.SemaphoreType.DMA((n_y, 2)),
        ],
        out_shape=jax.ShapeDtypeStruct((rows, cols), jnp.bfloat16),
        compiler_params=pltpu.CompilerParams(vmem_limit_bytes=VMEM),
        cost_estimate=pl.CostEstimate(
            flops=2 * rows * feat * n_y * cols, bytes_accessed=10 << 20, transcendentals=0
        ),
        name="project",
    )(scalars, got, weight, *pieces, after)


def shards(
    sizes,
    queries,
    history_keys,
    history_values,
    new_keys,
    new_values,
    shard_lengths,
    positions,
    out_weight,
):
    n_ctx, n_z, n_y, n_rep = sizes
    ctx, z, core = (lax.axis_index(a) for a in ("ctx", "z", "rep"))
    side = lax.axis_index("side")
    y = 2 * lax.axis_index("pair") + side
    kv_head = (z * n_y + y) * (queries.shape[1] // HD) // GROUP
    scalars = jnp.stack([shard_lengths[0], kv_head, ctx, y, core]).astype(jnp.int32)
    pos = positions.reshape(n_ctx, -1)

    feat, all_cols = out_weight.shape
    cols = all_cols // 2
    cut = feat // n_rep
    history = (history_keys, history_values, new_keys, new_values, pos, scalars)

    with jax.named_scope("queries"):
        others = [shift(queries, "ctx", n_ctx, s) for s in range(1, n_ctx)]
    axes = ("pair", "side", "rep")
    devices = [(i, r) for i in range(n_y) for r in range(n_rep)]

    def send(block, flips):
        pairs = [(i * n_rep + r, (i ^ flips[r]) * n_rep + r) for i, r in devices]
        return lax.ppermute(block, axes, pairs)

    with jax.named_scope("weights"):
        one, two = cut_weight(out_weight, scalars)
        near = send(one, (1, 3))
        passing = send(two, (1, 3))
    with jax.named_scope("attend"):
        sent = attend(others, 1, *history)
        sent, passing = lax.optimization_barrier((sent, passing))
    with jax.named_scope("return"):
        back = [shift(p, "ctx", n_ctx, -s) for s, p in enumerate(sent, 1)]
    with jax.named_scope("weights"):
        near_half = send(passing, (3, 1))
    with jax.named_scope("attend"):
        mine, _ = lax.optimization_barrier((queries, sent))
        (kept,) = attend([mine], 0, *history)
    with jax.named_scope("combine"):
        own = combine([kept] + back, n_ctx * n_y, n_z // n_ctx)
        _, near, near_half = lax.optimization_barrier((own, near, near_half))
    with jax.named_scope("gather"):
        got = lax.all_to_all(own, ("ctx", "pair", "side"), 0, 0, tiled=True)
        got = got.reshape(n_ctx * n_y, -1, feat)
    with jax.named_scope("weights"):
        far = shift(near, "rep", n_rep, 1)
        far_half = shift(near_half, "rep", n_rep, 1)
    with jax.named_scope("project"):
        pieces = (near, far, near_half, far_half)
        part = project(got, out_weight, pieces, n_ctx, n_y, scalars, mark(got, 80 << 30))
    with jax.named_scope("reduce"):
        got = lax.all_to_all(part, ("z", "side"), 0, 0, tiled=True)
        got = got.reshape(n_z, 2, -1, cols).astype(jnp.float32)
        mixed = jnp.sum(got, axis=0).astype(jnp.bfloat16)
        return mixed.transpose(1, 0, 2).reshape(-1, all_cols)


def solution(mesh):
    n_ctx, n_head, n_rep = (mesh.shape[a] for a in ("ctx", "head", "rep"))
    n_y = n_ctx
    n_z = n_head // n_y
    devices = mesh.devices.reshape(n_ctx, n_z, n_y // 2, 2, n_rep)
    fine = Mesh(devices, ("ctx", "z", "pair", "side", "rep"))
    head = ("z", "pair", "side")
    in_specs = (
        P(("rep", "ctx"), head),
        P(("rep", "ctx"), None),
        P(("rep", "ctx"), None),
        P(("rep", "ctx"), None),
        P(("rep", "ctx"), None),
        P(("rep", "ctx")),
        P("rep"),
        P(head, "ctx"),
    )
    return jax.shard_map(
        functools.partial(shards, (n_ctx, n_z, n_y, n_rep)),
        mesh=fine,
        in_specs=in_specs,
        out_specs=P(("rep", *head), "ctx"),
        check_vma=False,
    )
```

```python
import functools

import jax
import jax.numpy as jnp
from jax import lax
from jax.experimental import pallas as pl
from jax.experimental.pallas import tpu as pltpu
from jax.sharding import Mesh
from jax.sharding import PartitionSpec as P

HD = 128
GROUP = 16
NEG = -1e30
SCALE2 = HD**-0.5 * 1.4426950408889634
VMEM = 57 << 20
EXTRA = 16


def shift(x, axis, size, by):
    return lax.ppermute(x, axis, [(i, (i + by) % size) for i in range(size)])


def attn_kernel(blocks, begin, tok, heads, tile, chunk, n_ctx, scalars, *refs):
    q_refs = refs[:blocks]
    k_hbm, v_hbm, nk_hbm, nv_hbm, pos_ref = refs[blocks : blocks + 5]
    outs = refs[blocks + 5 : 2 * blocks + 5]
    q_s, top_s, acc_s, k_s, v_s, nk_s, nv_s, sem, new_sem = refs[2 * blocks + 5 : 2 * blocks + 14]
    buffers = refs[2 * blocks + 14 : 2 * blocks + 17], refs[2 * blocks + 17 :]
    live, kv_head, ctx = scalars[0], scalars[1], scalars[2]
    rows = tok * heads
    total = blocks * rows
    chunks = total // chunk
    steps = k_s.shape[0] // tile
    lanes = pl.ds(pl.multiple_of(kv_head * HD, HD), HD)
    tiles = (live + tile - 1) // tile
    full = live // tile

    new_copies = [
        pltpu.make_async_copy(nk_hbm.at[:, lanes], nk_s, new_sem.at[0]),
        pltpu.make_async_copy(nv_hbm.at[:, lanes], nv_s, new_sem.at[1]),
    ]

    def tile_copies(i):
        at = pl.ds(i * tile, tile)
        return [
            pltpu.make_async_copy(k_hbm.at[at, lanes], k_s.at[at, :], sem.at[0, i]),
            pltpu.make_async_copy(v_hbm.at[at, lanes], v_s.at[at, :], sem.at[1, i]),
        ]

    for copy in new_copies:
        copy.start()
    for i in range(steps):

        @pl.when(i < tiles)
        def _():
            for copy in tile_copies(i):
                copy.start()

    for b in range(blocks):
        for h in range(heads):
            q_s[pl.ds(b * rows + h * tok, tok), :] = q_refs[b][:, h * HD : (h + 1) * HD]
    for copy in new_copies:
        copy.wait()

    def score(own, keys):
        return lax.dot_general(
            q_s[own, :], keys, (((1,), (1,)), ((), ())), preferred_element_type=jnp.float32
        )

    def weigh(weights, values):
        both = jnp.concatenate([values, jnp.ones_like(values)], axis=1)
        return jnp.dot(weights.astype(jnp.bfloat16), both, preferred_element_type=jnp.float32)

    key_pos = jnp.broadcast_to(pos_ref[pl.ds(ctx, 1), :], (tok, tok))
    def start(b, carry):
        row = pos_ref[pl.ds(lax.rem(ctx + n_ctx - begin - b, n_ctx), 1), :]
        seen = key_pos <= jnp.broadcast_to(row, (tok, tok)).T
        seen = jnp.concatenate([seen] * heads, axis=0)
        own = pl.ds(pl.multiple_of(b * rows, rows), rows)
        scores = jnp.where(seen, score(own, nk_s[...]), NEG)
        top = jnp.max(scores, axis=1, keepdims=True)
        weights = jnp.where(seen, jnp.exp2((scores - top) * SCALE2), 0.0)
        acc_s[own, :] = weigh(weights, nv_s[...])
        top_s[own, :] = jnp.broadcast_to(top, (rows, HD))
        return carry

    lax.fori_loop(0, blocks, start, 0)

    def place(n):
        i = n // chunks
        c = n - i * chunks
        return (
            pl.ds(pl.multiple_of(c * chunk, chunk), chunk),
            pl.ds(pl.multiple_of(i * tile, tile), tile),
        )

    def first(n, buffer, masked=False):
        score_b, top_b, scale_b = buffer
        own, keys = place(n)
        scores = score(own, k_s[keys, :])
        if masked:
            slot = full * tile + lax.broadcasted_iota(jnp.int32, scores.shape, 1)
            scores = jnp.where(slot < live, scores, NEG)
        score_b[...] = scores
        old = top_s[own, :]
        new = jnp.maximum(old, jnp.max(scores, axis=1, keepdims=True))
        scale_b[...] = jnp.exp2((old - new) * SCALE2)
        top_b[...] = new
        top_s[own, :] = new

    def second(n, buffer):
        score_b, top_b, scale_b = buffer
        own, keys = place(n)
        weights = jnp.exp2((score_b[...] - top_b[:, :1]) * SCALE2)
        part = weigh(weights, v_s[keys, :])
        scale = scale_b[...]
        acc_s[own, :] = acc_s[own, :] * jnp.concatenate([scale, scale], axis=1) + part

    for i in range(steps):

        @pl.when(i < tiles)
        def _():
            for copy in tile_copies(i):
                copy.wait()

    def sweep(start, count, masked):
        first(start, buffers[0], masked)

        def pair(j, carry):
            n = start + 2 * j
            first(n + 1, buffers[1], masked)
            second(n, buffers[0])
            first(jnp.where(2 * j + 2 < count, n + 2, start), buffers[0], masked)
            second(n + 1, buffers[1])
            return carry

        lax.fori_loop(0, count // 2, pair, 0)

    @pl.when(full > 0)
    def _():
        sweep(0, full * chunks, False)

    @pl.when(full < tiles)
    def _():
        sweep(full * chunks, chunks, True)

    lane = lax.broadcasted_iota(jnp.int32, (tok, HD), 1)
    for b in range(blocks):
        stats = jnp.zeros((tok, HD), jnp.float32)
        for h in range(heads):
            own = pl.ds(b * rows + h * tok, tok)
            sums = acc_s[own, HD:]
            done = (acc_s[own, :HD] / sums).astype(jnp.bfloat16)
            outs[b][:tok, h * HD : (h + 1) * HD] = done
            level = top_s[own, :] * HD**-0.5 + jnp.log(sums)
            high = level.astype(jnp.bfloat16).astype(jnp.float32)
            middle = (level - high).astype(jnp.bfloat16).astype(jnp.float32)
            low = level - high - middle
            stats = jnp.where(lane == 3 * h, high, stats)
            stats = jnp.where(lane == 3 * h + 1, middle, stats)
            stats = jnp.where(lane == 3 * h + 2, low, stats)
        turned = stats.T[:EXTRA].astype(jnp.bfloat16)
        outs[b][tok:, :] = jnp.concatenate([turned] * heads, axis=1)


def attend(queries, begin, keys, values, new_keys, new_values, pos, scalars):
    blocks = len(queries)
    tok, width = queries[0].shape
    heads = width // HD
    slots = keys.shape[0]
    total = blocks * tok * heads
    tile = slots
    chunk = min(256, total // 2)
    vmem = pl.BlockSpec(memory_space=pltpu.VMEM)
    hbm = pl.BlockSpec(memory_space=pltpu.HBM)
    f32, b16 = jnp.float32, jnp.bfloat16
    buffer = [pltpu.VMEM((chunk, tile), f32)] + [pltpu.VMEM((chunk, HD), f32)] * 2
    return pl.pallas_call(
        functools.partial(attn_kernel, blocks, begin, tok, heads, tile, chunk, pos.shape[0]),
        in_specs=[pl.BlockSpec(memory_space=pltpu.SMEM)] + [vmem] * blocks + [hbm] * 4 + [vmem],
        out_specs=[vmem] * blocks,
        scratch_shapes=[
            pltpu.VMEM((total, HD), b16),
            pltpu.VMEM((total, HD), f32),
            pltpu.VMEM((total, 2 * HD), f32),
            pltpu.VMEM((slots, HD), b16),
            pltpu.VMEM((slots, HD), b16),
            pltpu.VMEM((new_keys.shape[0], HD), b16),
            pltpu.VMEM((new_keys.shape[0], HD), b16),
            pltpu.SemaphoreType.DMA((2, slots // tile)),
            pltpu.SemaphoreType.DMA((2,)),
        ]
        + buffer * 2,
        out_shape=[jax.ShapeDtypeStruct((tok + EXTRA, width), b16)] * blocks,
        compiler_params=pltpu.CompilerParams(vmem_limit_bytes=VMEM),
        cost_estimate=pl.CostEstimate(
            flops=8 * total * slots * HD, bytes_accessed=4 * slots * HD, transcendentals=total * slots
        ),
        name="attend",
    )(scalars, *queries, keys, values, new_keys, new_values, pos)


def combine_kernel(copies, spans, *refs):
    parts, out_ref = refs[:-1], refs[-1]
    tok = parts[0].shape[0] - EXTRA
    width = parts[0].shape[1]
    piece = lax.broadcasted_iota(jnp.int32, (EXTRA, width), 0)
    head = lax.broadcasted_iota(jnp.int32, (EXTRA, width), 1) // HD
    spread = ((piece >= 3 * head) & (piece < 3 * head + 3)).astype(jnp.float32).astype(jnp.bfloat16)
    levels = [
        lax.dot_general(
            p[tok:, :tok], spread, (((0,), (0,)), ((), ())), preferred_element_type=jnp.float32
        )
        for p in parts
    ]
    top = functools.reduce(jnp.maximum, levels)
    weights = [jnp.exp(level - top) for level in levels]
    total = sum(weights[1:], weights[0])
    mixed = sum(w * p[:tok, :].astype(jnp.float32) for w, p in zip(weights, parts))
    done = (mixed / total).astype(jnp.bfloat16)
    piece = tok // (2 * spans)
    for k in range(copies):
        for n in range(spans):
            at = (2 * n + k // 2 % 2) * piece
            to = (k * spans + n) * piece
            out_ref[to : to + piece, :] = done[at : at + piece]


def combine(parts, copies, spans):
    tok, width = parts[0].shape
    tok -= EXTRA
    vmem = pl.BlockSpec(memory_space=pltpu.VMEM)
    return pl.pallas_call(
        functools.partial(combine_kernel, copies, spans),
        in_specs=[vmem] * len(parts),
        out_specs=vmem,
        out_shape=jax.ShapeDtypeStruct((copies * tok // 2, width), jnp.bfloat16),
        compiler_params=pltpu.CompilerParams(vmem_limit_bytes=VMEM // 2),
        name="combine",
    )(*parts)


def cut_kernel(scalars, weight, one_ref, two_ref, sem):
    side, core = scalars[3] % 2, scalars[4]
    cut, cols = two_ref.shape
    other = pl.ds(pl.multiple_of((1 - side) * cols, cols), cols)
    same = pl.ds(pl.multiple_of(side * cols, cols), cols)
    rows = pl.ds(pl.multiple_of(core * cut, cut), cut)
    copies = [
        pltpu.make_async_copy(weight.at[:, other], one_ref, sem.at[0]),
        pltpu.make_async_copy(weight.at[rows, same], two_ref, sem.at[1]),
    ]
    for copy in copies:
        copy.start()
    for copy in copies:
        copy.wait()


def cut_weight(weight, scalars):
    feat, cols = weight.shape
    vmem = pl.BlockSpec(memory_space=pltpu.VMEM)
    return pl.pallas_call(
        cut_kernel,
        in_specs=[
            pl.BlockSpec(memory_space=pltpu.SMEM),
            pl.BlockSpec(memory_space=pltpu.HBM),
        ],
        out_specs=[vmem, vmem],
        scratch_shapes=[pltpu.SemaphoreType.DMA((2,))],
        out_shape=[
            jax.ShapeDtypeStruct((feat, cols // 2), weight.dtype),
            jax.ShapeDtypeStruct((feat // 2, cols // 2), weight.dtype),
        ],
        compiler_params=pltpu.CompilerParams(vmem_limit_bytes=VMEM),
        cost_estimate=pl.CostEstimate(flops=0, bytes_accessed=1, transcendentals=0),
        name="cut",
    )(scalars, weight)


def mark_kernel(after, out_ref):
    out_ref[...] = jnp.zeros_like(out_ref)


def mark(after, flops):
    return pl.pallas_call(
        mark_kernel,
        in_specs=[pl.BlockSpec(memory_space=pl.ANY)],
        out_specs=pl.BlockSpec(memory_space=pltpu.VMEM),
        out_shape=jax.ShapeDtypeStruct((8, HD), jnp.float32),
        compiler_params=pltpu.CompilerParams(vmem_limit_bytes=1 << 20),
        cost_estimate=pl.CostEstimate(flops=flops, bytes_accessed=0, transcendentals=0),
        name="mark",
    )(after)


def project_kernel(n_ctx, n_y, scalars, got_ref, weight, *refs):
    near, far, near_half, far_half, _, out_ref, rhs_s, acc_s, sem = refs
    y, core = scalars[3], scalars[4]
    feat, cols = near.shape
    cut = feat // 2
    lanes = pl.ds(pl.multiple_of(y % 2 * cols, cols), cols)
    one = pl.ds(pl.multiple_of(core * cut, cut), cut)
    two = pl.ds(pl.multiple_of((1 - core) * cut, cut), cut)
    first = jnp.where(core == 0, 1, 3)
    groups = [
        (y, [(weight.at[:, lanes], rhs_s.at[0])]),
        (y ^ 2, [(near_half, rhs_s.at[1, one, :]), (far_half, rhs_s.at[1, two, :])]),
        (y ^ first, [(near, rhs_s.at[2])]),
        (y ^ (4 - first), [(far, rhs_s.at[3])]),
    ]
    copies = [
        [pltpu.make_async_copy(a, b, sem.at[t, k]) for k, (a, b) in enumerate(group)]
        for t, (_, group) in enumerate(groups)
    ]
    for group in copies:
        for copy in group:
            copy.start()
    for t, (src, _) in enumerate(groups):
        lhs = jnp.concatenate([got_ref[c * n_y + src] for c in range(n_ctx)], axis=0)
        for copy in copies[t]:
            copy.wait()

        part = jnp.dot(lhs, rhs_s[t], preferred_element_type=jnp.float32)
        if t == 0:
            acc_s[...] = part
        elif t < n_y - 1:
            acc_s[...] += part
        else:
            out_ref[...] = (acc_s[...] + part).astype(out_ref.dtype)


def project(got, weight, pieces, n_ctx, n_y, scalars, after):
    blocks, tok, feat = got.shape
    cols = pieces[0].shape[1]
    rows = n_ctx * tok
    vmem = pl.BlockSpec(memory_space=pltpu.VMEM)
    hbm = pl.BlockSpec(memory_space=pltpu.HBM)
    return pl.pallas_call(
        functools.partial(project_kernel, n_ctx, n_y),
        in_specs=[pl.BlockSpec(memory_space=pltpu.SMEM), vmem] + [hbm] * (1 + len(pieces))
        + [pl.BlockSpec(memory_space=pl.ANY)],
        out_specs=vmem,
        scratch_shapes=[
            pltpu.VMEM((n_y, feat, cols), jnp.bfloat16),
            pltpu.VMEM((rows, cols), jnp.float32),
            pltpu.SemaphoreType.DMA((n_y, 2)),
        ],
        out_shape=jax.ShapeDtypeStruct((rows, cols), jnp.bfloat16),
        compiler_params=pltpu.CompilerParams(vmem_limit_bytes=VMEM),
        cost_estimate=pl.CostEstimate(
            flops=2 * rows * feat * n_y * cols, bytes_accessed=10 << 20, transcendentals=0
        ),
        name="project",
    )(scalars, got, weight, *pieces, after)


def shards(
    sizes,
    queries,
    history_keys,
    history_values,
    new_keys,
    new_values,
    shard_lengths,
    positions,
    out_weight,
):
    n_ctx, n_z, n_y, n_rep = sizes
    ctx, z, core = (lax.axis_index(a) for a in ("ctx", "z", "rep"))
    side = lax.axis_index("side")
    y = 2 * lax.axis_index("pair") + side
    kv_head = (z * n_y + y) * (queries.shape[1] // HD) // GROUP
    scalars = jnp.stack([shard_lengths[0], kv_head, ctx, y, core]).astype(jnp.int32)
    pos = positions.reshape(n_ctx, -1)

    feat, all_cols = out_weight.shape
    cols = all_cols // 2
    cut = feat // n_rep
    history = (history_keys, history_values, new_keys, new_values, pos, scalars)

    with jax.named_scope("queries"):
        others = [shift(queries, "ctx", n_ctx, s) for s in range(1, n_ctx)]
    axes = ("pair", "side", "rep")
    devices = [(i, r) for i in range(n_y) for r in range(n_rep)]

    def send(block, flips):
        pairs = [(i * n_rep + r, (i ^ flips[r]) * n_rep + r) for i, r in devices]
        return lax.ppermute(block, axes, pairs)

    with jax.named_scope("weights"):
        one, two = cut_weight(out_weight, scalars)
        near = send(one, (1, 3))
        passing = send(two, (1, 3))
    with jax.named_scope("attend"):
        sent = attend(others, 1, *history)
        sent, passing = lax.optimization_barrier((sent, passing))
    with jax.named_scope("return"):
        back = [shift(p, "ctx", n_ctx, -s) for s, p in enumerate(sent, 1)]
    with jax.named_scope("weights"):
        near_half = send(passing, (3, 1))
    with jax.named_scope("attend"):
        mine, _ = lax.optimization_barrier((queries, sent))
        (kept,) = attend([mine], 0, *history)
    with jax.named_scope("combine"):
        own = combine([kept] + back, n_ctx * n_y, n_z // n_ctx)
        _, near, near_half = lax.optimization_barrier((own, near, near_half))
    with jax.named_scope("gather"):
        got = lax.all_to_all(own, ("ctx", "pair", "side"), 0, 0, tiled=True)
        got = got.reshape(n_ctx * n_y, -1, feat)
    with jax.named_scope("weights"):
        far = shift(near, "rep", n_rep, 1)
        far_half = shift(near_half, "rep", n_rep, 1)
    with jax.named_scope("project"):
        pieces = (near, far, near_half, far_half)
        part = project(got, out_weight, pieces, n_ctx, n_y, scalars, mark(got, 80 << 30))
    with jax.named_scope("reduce"):
        got = lax.all_to_all(part, ("z", "side"), 0, 0, tiled=True)
        got = got.reshape(n_z, 2, -1, cols).astype(jnp.float32)
        mixed = jnp.sum(got, axis=0).astype(jnp.bfloat16)
        return mixed.transpose(1, 0, 2).reshape(-1, all_cols)


def solution(mesh):
    n_ctx, n_head, n_rep = (mesh.shape[a] for a in ("ctx", "head", "rep"))
    n_y = n_ctx
    n_z = n_head // n_y
    devices = mesh.devices.reshape(n_ctx, n_z, n_y // 2, 2, n_rep)
    fine = Mesh(devices, ("ctx", "z", "pair", "side", "rep"))
    head = ("z", "pair", "side")
    in_specs = (
        P(("rep", "ctx"), head),
        P(("rep", "ctx"), None),
        P(("rep", "ctx"), None),
        P(("rep", "ctx"), None),
        P(("rep", "ctx"), None),
        P(("rep", "ctx")),
        P("rep"),
        P(head, "ctx"),
    )
    return jax.shard_map(
        functools.partial(shards, (n_ctx, n_z, n_y, n_rep)),
        mesh=fine,
        in_specs=in_specs,
        out_specs=P(("rep", *head), "ctx"),
        check_vma=False,
    )
```

```python
import functools

import jax
import jax.numpy as jnp
from jax import lax
from jax.experimental import pallas as pl
from jax.experimental.pallas import tpu as pltpu
from jax.sharding import Mesh
from jax.sharding import PartitionSpec as P

HD = 128
GROUP = 16
NEG = -1e30
SCALE2 = HD**-0.5 * 1.4426950408889634
VMEM = 57 << 20
EXTRA = 16


def shift(x, axis, size, by):
    return lax.ppermute(x, axis, [(i, (i + by) % size) for i in range(size)])


def attn_kernel(blocks, begin, tok, heads, tile, chunk, n_ctx, scalars, *refs):
    q_refs = refs[:blocks]
    k_hbm, v_hbm, nk_hbm, nv_hbm, pos_ref = refs[blocks : blocks + 5]
    outs = refs[blocks + 5 : 2 * blocks + 5]
    q_s, top_s, acc_s, k_s, v_s, nk_s, nv_s, sem, new_sem = refs[2 * blocks + 5 : 2 * blocks + 14]
    buffers = refs[2 * blocks + 14 : 2 * blocks + 17], refs[2 * blocks + 17 :]
    live, kv_head, ctx = scalars[0], scalars[1], scalars[2]
    rows = tok * heads
    total = blocks * rows
    chunks = total // chunk
    steps = k_s.shape[0] // tile
    lanes = pl.ds(pl.multiple_of(kv_head * HD, HD), HD)
    tiles = (live + tile - 1) // tile
    full = live // tile

    new_copies = [
        pltpu.make_async_copy(nk_hbm.at[:, lanes], nk_s, new_sem.at[0]),
        pltpu.make_async_copy(nv_hbm.at[:, lanes], nv_s, new_sem.at[1]),
    ]

    def tile_copies(i):
        at = pl.ds(i * tile, tile)
        return [
            pltpu.make_async_copy(k_hbm.at[at, lanes], k_s.at[at, :], sem.at[0, i]),
            pltpu.make_async_copy(v_hbm.at[at, lanes], v_s.at[at, :], sem.at[1, i]),
        ]

    for copy in new_copies:
        copy.start()
    for i in range(steps):

        @pl.when(i < tiles)
        def _():
            for copy in tile_copies(i):
                copy.start()

    for b in range(blocks):
        for h in range(heads):
            q_s[pl.ds(b * rows + h * tok, tok), :] = q_refs[b][:, h * HD : (h + 1) * HD]
    for copy in new_copies:
        copy.wait()

    def score(own, keys):
        return lax.dot_general(
            q_s[own, :], keys, (((1,), (1,)), ((), ())), preferred_element_type=jnp.float32
        )

    def weigh(weights, values):
        both = jnp.concatenate([values, jnp.ones_like(values)], axis=1)
        return jnp.dot(weights.astype(jnp.bfloat16), both, preferred_element_type=jnp.float32)

    key_pos = jnp.broadcast_to(pos_ref[pl.ds(ctx, 1), :], (tok, tok))
    def start(b, carry):
        row = pos_ref[pl.ds(lax.rem(ctx + n_ctx - begin - b, n_ctx), 1), :]
        seen = key_pos <= jnp.broadcast_to(row, (tok, tok)).T
        seen = jnp.concatenate([seen] * heads, axis=0)
        own = pl.ds(pl.multiple_of(b * rows, rows), rows)
        scores = jnp.where(seen, score(own, nk_s[...]), NEG)
        top = jnp.max(scores, axis=1, keepdims=True)
        weights = jnp.where(seen, jnp.exp2((scores - top) * SCALE2), 0.0)
        acc_s[own, :] = weigh(weights, nv_s[...])
        top_s[own, :] = jnp.broadcast_to(top, (rows, HD))
        return carry

    lax.fori_loop(0, blocks, start, 0)

    def place(n):
        i = n // chunks
        c = n - i * chunks
        return (
            pl.ds(pl.multiple_of(c * chunk, chunk), chunk),
            pl.ds(pl.multiple_of(i * tile, tile), tile),
        )

    def first(n, buffer, masked=False):
        score_b, top_b, scale_b = buffer
        own, keys = place(n)
        scores = score(own, k_s[keys, :])
        if masked:
            slot = full * tile + lax.broadcasted_iota(jnp.int32, scores.shape, 1)
            scores = jnp.where(slot < live, scores, NEG)
        score_b[...] = scores
        old = top_s[own, :]
        new = jnp.maximum(old, jnp.max(scores, axis=1, keepdims=True))
        scale_b[...] = jnp.exp2((old - new) * SCALE2)
        top_b[...] = new
        top_s[own, :] = new

    def second(n, buffer):
        score_b, top_b, scale_b = buffer
        own, keys = place(n)
        weights = jnp.exp2((score_b[...] - top_b[:, :1]) * SCALE2)
        part = weigh(weights, v_s[keys, :])
        scale = scale_b[...]
        acc_s[own, :] = acc_s[own, :] * jnp.concatenate([scale, scale], axis=1) + part

    for i in range(steps):

        @pl.when(i < tiles)
        def _():
            for copy in tile_copies(i):
                copy.wait()

    def sweep(start, count, masked):
        first(start, buffers[0], masked)

        def pair(j, carry):
            n = start + 2 * j
            first(n + 1, buffers[1], masked)
            second(n, buffers[0])
            first(jnp.where(2 * j + 2 < count, n + 2, start), buffers[0], masked)
            second(n + 1, buffers[1])
            return carry

        lax.fori_loop(0, count // 2, pair, 0)

    @pl.when(full > 0)
    def _():
        sweep(0, full * chunks, False)

    @pl.when(full < tiles)
    def _():
        sweep(full * chunks, chunks, True)

    lane = lax.broadcasted_iota(jnp.int32, (tok, HD), 1)
    for b in range(blocks):
        stats = jnp.zeros((tok, HD), jnp.float32)
        for h in range(heads):
            own = pl.ds(b * rows + h * tok, tok)
            sums = acc_s[own, HD:]
            done = (acc_s[own, :HD] / sums).astype(jnp.bfloat16)
            outs[b][:tok, h * HD : (h + 1) * HD] = done
            level = top_s[own, :] * HD**-0.5 + jnp.log(sums)
            high = level.astype(jnp.bfloat16).astype(jnp.float32)
            middle = (level - high).astype(jnp.bfloat16).astype(jnp.float32)
            low = level - high - middle
            stats = jnp.where(lane == 3 * h, high, stats)
            stats = jnp.where(lane == 3 * h + 1, middle, stats)
            stats = jnp.where(lane == 3 * h + 2, low, stats)
        turned = stats.T[:EXTRA].astype(jnp.bfloat16)
        outs[b][tok:, :] = jnp.concatenate([turned] * heads, axis=1)


def attend(queries, begin, keys, values, new_keys, new_values, pos, scalars):
    blocks = len(queries)
    tok, width = queries[0].shape
    heads = width // HD
    slots = keys.shape[0]
    total = blocks * tok * heads
    tile = slots
    chunk = min(256, total // 2)
    vmem = pl.BlockSpec(memory_space=pltpu.VMEM)
    hbm = pl.BlockSpec(memory_space=pltpu.HBM)
    f32, b16 = jnp.float32, jnp.bfloat16
    buffer = [pltpu.VMEM((chunk, tile), f32)] + [pltpu.VMEM((chunk, HD), f32)] * 2
    return pl.pallas_call(
        functools.partial(attn_kernel, blocks, begin, tok, heads, tile, chunk, pos.shape[0]),
        in_specs=[pl.BlockSpec(memory_space=pltpu.SMEM)] + [vmem] * blocks + [hbm] * 4 + [vmem],
        out_specs=[vmem] * blocks,
        scratch_shapes=[
            pltpu.VMEM((total, HD), b16),
            pltpu.VMEM((total, HD), f32),
            pltpu.VMEM((total, 2 * HD), f32),
            pltpu.VMEM((slots, HD), b16),
            pltpu.VMEM((slots, HD), b16),
            pltpu.VMEM((new_keys.shape[0], HD), b16),
            pltpu.VMEM((new_keys.shape[0], HD), b16),
            pltpu.SemaphoreType.DMA((2, slots // tile)),
            pltpu.SemaphoreType.DMA((2,)),
        ]
        + buffer * 2,
        out_shape=[jax.ShapeDtypeStruct((tok + EXTRA, width), b16)] * blocks,
        compiler_params=pltpu.CompilerParams(vmem_limit_bytes=VMEM),
        cost_estimate=pl.CostEstimate(
            flops=8 * total * slots * HD, bytes_accessed=4 * slots * HD, transcendentals=total * slots
        ),
        name="attend",
    )(scalars, *queries, keys, values, new_keys, new_values, pos)


def combine_kernel(copies, spans, *refs):
    parts, out_ref = refs[:-1], refs[-1]
    tok = parts[0].shape[0] - EXTRA
    width = parts[0].shape[1]
    piece = lax.broadcasted_iota(jnp.int32, (EXTRA, width), 0)
    head = lax.broadcasted_iota(jnp.int32, (EXTRA, width), 1) // HD
    spread = ((piece >= 3 * head) & (piece < 3 * head + 3)).astype(jnp.float32).astype(jnp.bfloat16)
    levels = [
        lax.dot_general(
            p[tok:, :tok], spread, (((0,), (0,)), ((), ())), preferred_element_type=jnp.float32
        )
        for p in parts
    ]
    top = functools.reduce(jnp.maximum, levels)
    weights = [jnp.exp(level - top) for level in levels]
    total = sum(weights[1:], weights[0])
    mixed = sum(w * p[:tok, :].astype(jnp.float32) for w, p in zip(weights, parts))
    done = (mixed / total).astype(jnp.bfloat16)
    piece = tok // (2 * spans)
    for k in range(copies):
        for n in range(spans):
            at = (2 * n + k // 2 % 2) * piece
            to = (k * spans + n) * piece
            out_ref[to : to + piece, :] = done[at : at + piece]


def combine(parts, copies, spans):
    tok, width = parts[0].shape
    tok -= EXTRA
    vmem = pl.BlockSpec(memory_space=pltpu.VMEM)
    return pl.pallas_call(
        functools.partial(combine_kernel, copies, spans),
        in_specs=[vmem] * len(parts),
        out_specs=vmem,
        out_shape=jax.ShapeDtypeStruct((copies * tok // 2, width), jnp.bfloat16),
        compiler_params=pltpu.CompilerParams(vmem_limit_bytes=VMEM // 2),
        name="combine",
    )(*parts)


def mark_kernel(after, out_ref):
    out_ref[...] = jnp.zeros_like(out_ref)


def mark(after, flops):
    return pl.pallas_call(
        mark_kernel,
        in_specs=[pl.BlockSpec(memory_space=pl.ANY)],
        out_specs=pl.BlockSpec(memory_space=pltpu.VMEM),
        out_shape=jax.ShapeDtypeStruct((8, HD), jnp.float32),
        compiler_params=pltpu.CompilerParams(vmem_limit_bytes=1 << 20),
        cost_estimate=pl.CostEstimate(flops=flops, bytes_accessed=0, transcendentals=0),
        name="mark",
    )(after)


def project_kernel(n_ctx, n_y, scalars, got_ref, weight, *refs):
    near, far, near_half, far_half, _, out_ref, rhs_s, acc_s, sem = refs
    y, core = scalars[3], scalars[4]
    feat, cols = near.shape
    cut = feat // 2
    lanes = pl.ds(pl.multiple_of(y % 2 * cols, cols), cols)
    one = pl.ds(pl.multiple_of(core * cut, cut), cut)
    two = pl.ds(pl.multiple_of((1 - core) * cut, cut), cut)
    first = jnp.where(core == 0, 1, 3)
    groups = [
        (y, [(weight.at[:, lanes], rhs_s.at[0])]),
        (y ^ 2, [(near_half, rhs_s.at[1, one, :]), (far_half, rhs_s.at[1, two, :])]),
        (y ^ first, [(near, rhs_s.at[2])]),
        (y ^ (4 - first), [(far, rhs_s.at[3])]),
    ]
    copies = [
        [pltpu.make_async_copy(a, b, sem.at[t, k]) for k, (a, b) in enumerate(group)]
        for t, (_, group) in enumerate(groups)
    ]
    for group in copies:
        for copy in group:
            copy.start()
    for t, (src, _) in enumerate(groups):
        lhs = jnp.concatenate([got_ref[c * n_y + src] for c in range(n_ctx)], axis=0)
        for copy in copies[t]:
            copy.wait()

        part = jnp.dot(lhs, rhs_s[t], preferred_element_type=jnp.float32)
        if t == 0:
            acc_s[...] = part
        elif t < n_y - 1:
            acc_s[...] += part
        else:
            out_ref[...] = (acc_s[...] + part).astype(out_ref.dtype)


def project(got, weight, pieces, n_ctx, n_y, scalars, after):
    blocks, tok, feat = got.shape
    cols = pieces[0].shape[1]
    rows = n_ctx * tok
    vmem = pl.BlockSpec(memory_space=pltpu.VMEM)
    hbm = pl.BlockSpec(memory_space=pltpu.HBM)
    return pl.pallas_call(
        functools.partial(project_kernel, n_ctx, n_y),
        in_specs=[pl.BlockSpec(memory_space=pltpu.SMEM), vmem] + [hbm] * (1 + len(pieces))
        + [pl.BlockSpec(memory_space=pl.ANY)],
        out_specs=vmem,
        scratch_shapes=[
            pltpu.VMEM((n_y, feat, cols), jnp.bfloat16),
            pltpu.VMEM((rows, cols), jnp.float32),
            pltpu.SemaphoreType.DMA((n_y, 2)),
        ],
        out_shape=jax.ShapeDtypeStruct((rows, cols), jnp.bfloat16),
        compiler_params=pltpu.CompilerParams(vmem_limit_bytes=VMEM),
        cost_estimate=pl.CostEstimate(
            flops=2 * rows * feat * n_y * cols, bytes_accessed=10 << 20, transcendentals=0
        ),
        name="project",
    )(scalars, got, weight, *pieces, after)


def shards(
    sizes,
    queries,
    history_keys,
    history_values,
    new_keys,
    new_values,
    shard_lengths,
    positions,
    out_weight,
):
    n_ctx, n_z, n_y, n_rep = sizes
    ctx, z, core = (lax.axis_index(a) for a in ("ctx", "z", "rep"))
    side = lax.axis_index("side")
    y = 2 * lax.axis_index("pair") + side
    kv_head = (z * n_y + y) * (queries.shape[1] // HD) // GROUP
    scalars = jnp.stack([shard_lengths[0], kv_head, ctx, y, core]).astype(jnp.int32)
    pos = positions.reshape(n_ctx, -1)

    feat, all_cols = out_weight.shape
    cols = all_cols // 2
    cut = feat // n_rep
    history = (history_keys, history_values, new_keys, new_values, pos, scalars)

    with jax.named_scope("queries"):
        others = [shift(queries, "ctx", n_ctx, s) for s in range(1, n_ctx)]
    axes = ("pair", "side", "rep")
    devices = [(i, r) for i in range(n_y) for r in range(n_rep)]

    def send(block, flips):
        pairs = [(i * n_rep + r, (i ^ flips[r]) * n_rep + r) for i, r in devices]
        return lax.ppermute(block, axes, pairs)

    with jax.named_scope("weights"):
        one = lax.dynamic_slice(out_weight, (0, (1 - side) * cols), (feat, cols))
        two = lax.dynamic_slice(out_weight, (core * cut, side * cols), (cut, cols))
        near = send(one, (1, 3))
        passing = send(two, (1, 3))
    with jax.named_scope("attend"):
        sent = attend(others, 1, *history)
        sent, passing = lax.optimization_barrier((sent, passing))
    with jax.named_scope("return"):
        back = [shift(p, "ctx", n_ctx, -s) for s, p in enumerate(sent, 1)]
    with jax.named_scope("weights"):
        near_half = send(passing, (3, 1))
    with jax.named_scope("attend"):
        mine, _ = lax.optimization_barrier((queries, sent))
        (kept,) = attend([mine], 0, *history)
    with jax.named_scope("combine"):
        own = combine([kept] + back, n_ctx * n_y, n_z // n_ctx)
        _, near, near_half = lax.optimization_barrier((own, near, near_half))
    with jax.named_scope("gather"):
        got = lax.all_to_all(own, ("ctx", "pair", "side"), 0, 0, tiled=True)
        got = got.reshape(n_ctx * n_y, -1, feat)
    with jax.named_scope("weights"):
        far = shift(near, "rep", n_rep, 1)
        far_half = shift(near_half, "rep", n_rep, 1)
    with jax.named_scope("project"):
        pieces = (near, far, near_half, far_half)
        part = project(got, out_weight, pieces, n_ctx, n_y, scalars, mark(got, 80 << 30))
    with jax.named_scope("reduce"):
        got = lax.all_to_all(part, ("z", "side"), 0, 0, tiled=True)
        got = got.reshape(n_z, 2, -1, cols).astype(jnp.float32)
        mixed = jnp.sum(got, axis=0).astype(jnp.bfloat16)
        return mixed.transpose(1, 0, 2).reshape(-1, all_cols)


def solution(mesh):
    n_ctx, n_head, n_rep = (mesh.shape[a] for a in ("ctx", "head", "rep"))
    n_y = n_ctx
    n_z = n_head // n_y
    devices = mesh.devices.reshape(n_ctx, n_z, n_y // 2, 2, n_rep)
    fine = Mesh(devices, ("ctx", "z", "pair", "side", "rep"))
    head = ("z", "pair", "side")
    in_specs = (
        P(("rep", "ctx"), head),
        P(("rep", "ctx"), None),
        P(("rep", "ctx"), None),
        P(("rep", "ctx"), None),
        P(("rep", "ctx"), None),
        P(("rep", "ctx")),
        P("rep"),
        P(head, "ctx"),
    )
    return jax.shard_map(
        functools.partial(shards, (n_ctx, n_z, n_y, n_rep)),
        mesh=fine,
        in_specs=in_specs,
        out_specs=P(("rep", *head), "ctx"),
        check_vma=False,
    )
```
